32 devices in a mesh: groups: 2 (over y), rows: 4 (over z), pipe: 2 (over x), cols: 2 (over core).
Axes of the slice: x: 2, y: 2, z: 4, core: 2. Of those that a mesh axis runs over, the one named last changes fastest.
Arguments:
- inputs: bfloat16 [8, 16, 256, 128], P(None, ('groups', 'rows'), 'cols'), parts along dimension 1, may hold values from -6 to 6
- hidden_init: bfloat16 [2, 16, 256, 128], P('pipe', ('groups', 'rows'), 'cols'), parts along dimension 1, may hold values from -3 to 3
- cell_init: float32 [2, 16, 256, 128], P('pipe', ('groups', 'rows'), 'cols'), parts along dimension 1, may hold values from -4 to 4
- kernels: bfloat16 [2, 2304, 512], P('pipe'), may hold values from -0.5 to 2.5
- biases: float32 [2, 512], P('pipe'), may hold values from -3 to 4.25
Outputs:
- hidden_seq: bfloat16 [2, 8, 16, 256, 128], P('pipe', None, ('groups', 'rows'), 'cols'), parts along dimension 2
- cell_final: float32 [2, 16, 256, 128], P('pipe', ('groups', 'rows'), 'cols'), parts along dimension 1
The draws below stay inside these ranges and needn't reach their ends.
There are 2 independent parts, one for each index of `groups`. The reference program is written for one: setup_inputs(seed, part) draws one part's arguments, and reference() takes and returns one part's arrays. A program takes and returns all parts, laid end to end along the dimension named above; an argument that names none is the same for every part. Nothing has to cross between parts.
All inputs are finite; a program needn't handle non-finite values.
Results may differ from the reference program's by a relative error of at most 0.0038.
Values may be sent and summed in bfloat16 or wider, within the bound.
No kernel may reach another device: no remote copies, remote signals or barrier semaphores. Data moves between devices by JAX's collectives and lax.ppermute only.
A program may use at most 64 MiB of HBM per device.

```python
import jax
import jax.numpy as jnp

CH = 128
STEPS = 8
LAYERS = 2
H = 8
W = 256


def draw_kernels(key, part):
    key = jax.random.fold_in(key, 11)
    jitter_key = jax.random.fold_in(key, 1)
    order_key = jax.random.fold_in(key, 2)
    extent = (LAYERS, 18 * CH, 4 * CH)
    spread = (18.0 * CH) ** (-0.5)
    jitter = jnp.clip(jax.random.normal(jitter_key, extent, jnp.float32), -6.0, 6.0)
    orders = jax.vmap(lambda subkey: jax.random.permutation(subkey, CH))(jax.random.split(order_key, LAYERS))
    heading = orders % 4
    tap_of = jnp.where(heading == 0, 1, jnp.where(heading == 1, 7, jnp.where(heading == 2, 3, 5)))
    row_ids = jnp.arange(18 * CH)
    row_tap = row_ids // (2 * CH)
    within = row_ids % (2 * CH)
    channel = within - CH
    carried = within >= CH
    chosen = tap_of[:, jnp.clip(channel, 0, CH - 1)]
    row_live = jnp.logical_and(carried[None, :], chosen == row_tap[None, :])
    col_ids = jnp.arange(4 * CH)
    target = col_ids[None, :] == (2 * CH + channel)[:, None]
    transport = jnp.where(jnp.logical_and(row_live[:, :, None], target[None, :, :]), 2.0, 0.0)
    return (jitter * spread + transport).astype(jnp.bfloat16)


def draw_biases(key, part):
    key = jax.random.fold_in(key, 23)
    gate_block = jnp.arange(4 * CH) // CH
    centre = jnp.where(gate_block == 1, -0.5, jnp.where(gate_block == 2, 0.0, 3.0))
    spread = jnp.where(gate_block == 1, 1.0, jnp.where(gate_block == 2, 0.7, 0.5))
    jitter = jnp.clip(jax.random.normal(key, (LAYERS, 4 * CH), jnp.float32), -2.5, 2.5)
    return (centre[None, :] + spread[None, :] * jitter).astype(jnp.float32)


def block_scale(stream_key, shape, shards, least, largest):
    level = 1.0
    for axis_at, shards_of in shards:
        steps = jax.random.uniform(jax.random.fold_in(jax.random.fold_in(stream_key, 6), axis_at), (shards_of,), jnp.float32, least / len(shards), largest / len(shards))
        level = level * jnp.repeat(jnp.exp(steps), shape[axis_at] // shards_of).reshape((-1,) + (1,) * (len(shape) - 1 - axis_at))
    return level


def scatter_about(rng, dims, scale, most, shards=(), held_as=jnp.bfloat16):
    values = jax.random.normal(rng, dims, jnp.float32) * scale
    if len(shards) > 0:
        values = block_scale(rng, dims, shards, -0.22, 0.18) * values
    return jnp.clip(values, min=-most, max=most).astype(held_as)


def setup_inputs(seed: int = 0, part: int = 0) -> dict:
    key_of = jax.random.split(jax.random.key(seed), 6)
    part_keys = jax.random.split(jax.random.fold_in(key_of[5], part), 6)
    inputs = scatter_about(part_keys[0], (STEPS, H, W, CH), 1.0, 6.0, ((1, 4), (2, 2)))
    hidden_init = scatter_about(part_keys[1], (LAYERS, H, W, CH), 0.5, 3.0, ((0, 2), (1, 4), (2, 2)))
    cell_init = scatter_about(part_keys[2], (LAYERS, H, W, CH), 1.0, 4.0, ((0, 2), (1, 4), (2, 2)), jnp.float32)
    kernels = draw_kernels(jax.random.fold_in(key_of[5], 71), part)
    biases = draw_biases(jax.random.fold_in(key_of[5], 71), part)
    return dict(inputs=inputs, hidden_init=hidden_init, cell_init=cell_init, kernels=kernels, biases=biases)


def advance(x_map, hidden, cell_state, weights, bias_row):
    rows_n, cols_n, width = hidden.shape
    stacked = jnp.concatenate([x_map, hidden], -1)
    padded = jnp.pad(stacked, ((1, 1), (1, 1), (0, 0)))
    taps = [padded[row_off:row_off + rows_n, col_off:col_off + cols_n] for row_off in range(3) for col_off in range(3)]
    slab = jnp.concatenate(taps, -1).reshape(rows_n * cols_n, 18 * width)
    gates = jnp.dot(slab, weights, preferred_element_type=jnp.float32) + bias_row
    gates = gates.reshape(rows_n, cols_n, 4 * width)
    in_gate = jax.nn.sigmoid(gates[..., :width])
    forget = jax.nn.sigmoid(gates[..., width:2 * width])
    candidate = jnp.tanh(gates[..., 2 * width:3 * width])
    out_gate = jax.nn.sigmoid(gates[..., 3 * width:])
    new_cell = forget * cell_state + in_gate * candidate
    new_hidden = (out_gate * jnp.tanh(new_cell)).astype(jnp.bfloat16)
    return new_hidden, new_cell


def reference(inputs, hidden_init, cell_init, kernels, biases):
    layer_in = [inputs[number] for number in range(STEPS)]
    all_hidden = []
    all_cells = []
    for layer_no in range(LAYERS):
        hidden = hidden_init[layer_no]
        cell_state = cell_init[layer_no]
        produced = []
        for time_no in range(STEPS):
            hidden, cell_state = advance(layer_in[time_no], hidden, cell_state, kernels[layer_no], biases[layer_no])
            produced.append(hidden)
        layer_in = produced
        all_hidden.append(jnp.stack(produced, 0))
        all_cells.append(cell_state)
    return jnp.stack(all_hidden, 0), jnp.stack(all_cells, 0)
```

```python
import functools

import jax
import jax.numpy as jnp
from jax import lax
from jax.experimental import pallas as pl
from jax.experimental.pallas import tpu as pltpu
from jax.sharding import PartitionSpec as P

BF = jnp.bfloat16
F32 = jnp.float32


def round_up(value, unit):
    return -(-value // unit) * unit


def partner(index, hop, count):
    if count & (count - 1) == 0:
        return index ^ hop, index ^ hop
    return (index + hop) % count, (index + count - hop) % count


def sigmoid(value):
    return 0.5 * jnp.tanh(0.5 * value) + 0.5


def step_kernel(dims, step, first_layer, *refs):
    rows_n, band, width, wide, chans, steps, count, phase = dims
    place, refs = refs[0], list(refs[1:])
    maps_ref = None
    early = [refs.pop(0) for _ in range(count)] if step == 0 else None
    late = None
    if first_layer and step > 0:
        late = [refs.pop(0) for _ in range(count)]
    if not first_layer:
        maps_ref = refs.pop(0)
    hidden_ref = cell_ref = None
    if step > 0:
        hidden_ref, cell_ref = refs.pop(0), refs.pop(0)
    weights, bias, _ = refs[:3]
    hidden_out, cell_out, kept, slab = refs[3:]
    total = rows_n * width
    lip = (wide - width) // 2

    @pl.when(place[0] == phase)
    def _():
        blank = jnp.zeros((width, 6 * chans), BF)
        slab[0:width, :] = blank
        slab[total + width : total + 2 * width, :] = blank

        def spread(lane, value):
            value = value.astype(F32)
            for tap in range(3):
                moved = value if tap == 1 else pltpu.roll(value, (1 - tap) % total, 0)
                at = 2 * chans * tap + lane
                slab[width : width + total, at : at + chans] = moved.astype(BF)

        def spread_band(lane, value, source, extent):
            flat = value.reshape(band * extent, chans).astype(F32)
            edge = (extent - width) // 2
            for tap in range(3):
                moved = flat if tap == 1 else pltpu.roll(flat, (1 - tap) % (band * extent), 0)
                moved = moved.reshape(band, extent, chans)[:, edge : edge + width]
                moved = moved.reshape(band * width, chans).astype(BF)
                at = 2 * chans * tap + lane
                start = pl.multiple_of((source * band + 1) * width, 16)
                slab[pl.ds(start, band * width), at : at + chans] = moved

        if step == 0:
            for hop in range(count):
                source = place[2 + hop]
                spread_band(chans, early[hop][0], source, wide)
                if first_layer:
                    spread_band(0, early[hop][2], source, wide)
                start = pl.multiple_of(source * band * width, 16)
                cell = early[hop][1].astype(F32)[:, lip : lip + width]
                cell_out[pl.ds(start, band * width), :] = cell.reshape(band * width, chans)
        else:
            spread(chans, hidden_ref[...].reshape(total, chans))
            if first_layer:
                for hop in range(count):
                    spread_band(0, late[hop][...], place[2 + hop], width)
        if not first_layer:
            spread(0, maps_ref[...].reshape(total, chans))

        depth = 6 * chans
        gates = bias[...]
        for tap in range(3):
            gates = gates + jnp.dot(
                slab[tap * width : tap * width + total, :],
                weights[tap * depth : (tap + 1) * depth, :],
                preferred_element_type=F32,
            )
        cell = cell_out[...] if step == 0 else cell_ref[...]
        cell = sigmoid(gates[:, chans : 2 * chans]) * cell + sigmoid(gates[:, :chans]) * jnp.tanh(
            gates[:, 2 * chans : 3 * chans]
        )
        hidden = sigmoid(gates[:, 3 * chans :]) * jnp.tanh(cell)
        hidden = hidden.reshape(rows_n, width, chans)
        column = place[1] + lax.broadcasted_iota(jnp.int32, hidden.shape, 1)
        inside = jnp.logical_and(column >= 0, column < place[2 + count])
        hidden = jnp.where(inside, hidden, 0.0).astype(BF)
        hidden_out[...] = hidden
        cell_out[...] = cell
        kept[:, step] = hidden
        if step == steps - 1:
            high = cell.astype(BF)
            low = (cell - high.astype(F32)).astype(BF)
            kept[:, steps] = high.reshape(rows_n, width, chans)
            kept[:, steps + 1] = low.reshape(rows_n, width, chans)


def advance(dims, step, first_layer, place, sources, weights, bias, kept):
    rows_n, band, width, wide, chans, steps, count, phase = dims
    vmem = pl.BlockSpec(memory_space=pltpu.VMEM)
    operands = [place, *sources, weights, bias, kept]
    total = rows_n * width
    return pl.pallas_call(
        functools.partial(step_kernel, dims, step, first_layer),
        out_shape=(
            jax.ShapeDtypeStruct((rows_n, width, chans), BF),
            jax.ShapeDtypeStruct((total, chans), F32),
            jax.ShapeDtypeStruct(kept.shape, kept.dtype),
        ),
        in_specs=[pl.BlockSpec(memory_space=pltpu.SMEM)] + [vmem] * (len(operands) - 1),
        out_specs=(vmem, vmem, vmem),
        scratch_shapes=[pltpu.VMEM((total + 2 * width, 6 * chans), BF)],
        input_output_aliases={len(operands) - 1: 2},
        compiler_params=pltpu.CompilerParams(vmem_limit_bytes=40 * 1024 * 1024),
        cost_estimate=pl.CostEstimate(
            flops=2 * total * 18 * chans * 4 * chans,
            bytes_accessed=1000000,
            transcendentals=5 * total * chans,
        ),
    )(*operands)


def column_edges(block, extent):
    count = lax.axis_size("cols")
    place = lax.axis_index("cols")
    first, last = block[..., :extent, :], block[..., block.shape[-2] - extent :, :]
    if count == 2:
        got = lax.ppermute(jnp.where(place == 0, last, first), "cols", [(0, 1), (1, 0)])
        blank = jnp.zeros_like(got)
        left, right = jnp.where(place == 1, got, blank), jnp.where(place == 0, got, blank)
    else:
        left = lax.ppermute(last, "cols", [(n, n + 1) for n in range(count - 1)])
        right = lax.ppermute(first, "cols", [(n + 1, n) for n in range(count - 1)])
    return jnp.concatenate([left, block, right], axis=-2)


def exchange(piece_for, place, count):
    got = [piece_for(place)]
    for hop in range(1, count):
        target, _ = partner(place, hop, count)
        route = [(n, partner(n, hop, count)[0]) for n in range(count)]
        got.append(lax.ppermute(piece_for(target), "rows", route))
    return got


def shards(inputs, hidden_init, cell_init, kernels, biases):
    steps, band, columns, chans = inputs.shape
    count = lax.axis_size("rows")
    layers = lax.axis_size("pipe")
    place_row = lax.axis_index("rows")
    place_col = lax.axis_index("cols")
    layer = lax.axis_index("pipe")
    rows_n = band * count
    strip = columns // count
    pad = round_up(steps + layers - 2, 8)
    width = round_up(strip + 2 * pad, 16)
    wide = width + 16
    edge = round_up(max(pad + 8, width - pad + 8 - strip), 16)

    maps = jnp.concatenate([hidden_init, cell_init.astype(BF), inputs], axis=0)
    padded = column_edges(maps, edge)

    def cut(first, last, reach, extent):
        def piece_for(index):
            start = index * strip + (edge - reach)
            return lax.dynamic_slice_in_dim(padded[first:last], start, extent, axis=2)

        return exchange(piece_for, place_row, count)

    early = cut(0, 3, pad + 8, wide)
    middle = (steps + 1) // 2
    late_a = cut(3, 2 + middle, pad, width)
    late_b = cut(2 + middle, 2 + steps, pad, width)

    sources = [partner(place_row, hop, count)[1] for hop in range(count)]
    first_column = place_col * columns + place_row * strip - pad
    everything = columns * lax.axis_size("cols")
    place = jnp.stack([layer, first_column, *sources, jnp.asarray(everything)]).astype(jnp.int32)

    kept = jnp.zeros((rows_n, steps + 2, width, chans), BF)
    weights, bias = kernels[0], biases
    sent = []
    for phase in range(layers):
        dims = (rows_n, band, width, wide, chans, steps, count, phase)
        received = sent
        sent = []
        hidden = cell = None
        for step in range(steps):
            feed = []
            if step == 0:
                feed += early
            if phase == 0 and step > 0:
                late, at = (late_a, step - 1) if step < middle else (late_b, step - middle)
                feed += [piece[at] for piece in late]
            if phase > 0:
                feed.append(received[step])
            if step > 0:
                feed += [hidden, cell]
            hidden, cell, kept = advance(
                dims, step, phase == 0, place, feed, weights, bias, kept
            )
            if phase < layers - 1:
                sent.append(lax.ppermute(hidden, "pipe", [(phase, phase + 1)]))

    def out_piece(index):
        piece = lax.dynamic_slice_in_dim(kept, index * band, band, axis=0)
        return piece[:, :, pad : pad + strip]

    out = jnp.zeros((band, steps + 2, columns, chans), BF)
    for source, piece in zip(sources, exchange(out_piece, place_row, count)):
        out = lax.dynamic_update_slice_in_dim(out, piece, source * strip, axis=2)
    produced = jnp.swapaxes(out[:, :steps], 0, 1)
    final = out[:, steps].astype(F32) + out[:, steps + 1].astype(F32)
    return produced[None], final[None]


def solution(mesh):
    return jax.shard_map(
        shards,
        mesh=mesh,
        in_specs=(
            P(None, ("groups", "rows"), "cols", None),
            P("pipe", ("groups", "rows"), "cols", None),
            P("pipe", ("groups", "rows"), "cols", None),
            P("pipe", None, None),
            P("pipe", None),
        ),
        out_specs=(
            P("pipe", None, ("groups", "rows"), "cols", None),
            P("pipe", ("groups", "rows"), "cols", None),
        ),
        check_vma=False,
    )
```

```python
import functools

import jax
import jax.numpy as jnp
from jax import lax
from jax.experimental import pallas as pl
from jax.experimental.pallas import tpu as pltpu
from jax.sharding import PartitionSpec as P

BF = jnp.bfloat16
F32 = jnp.float32
CHUNK = 1
LAG = 3
FIRST = 3
VMEM_LIMIT = 24 * 1024 * 1024


def round_up(value, unit):
    return -(-value // unit) * unit


def partner(index, hop, count):
    if count & (count - 1) == 0:
        return index ^ hop, index ^ hop
    return (index + hop) % count, (index + count - hop) % count


def sigmoid(value):
    return 0.5 * jnp.tanh(0.5 * value) + 0.5


class Piece:
    def __init__(self, strip, need, begin, band):
        self.extent = round_up(strip + 2 * need, 8)
        self.left = (self.extent - strip) // 2
        self.begin = begin
        self.end = begin + band * self.extent


class Plan:
    def __init__(self, inputs):
        self.steps, self.band, self.columns, self.chans = inputs.shape
        self.count = lax.axis_size("rows")
        self.cols = lax.axis_size("cols")
        self.layers = lax.axis_size("pipe")
        self.grid_columns = self.columns * self.cols
        self.rows_n = self.band * self.count
        self.strip = self.columns // self.count
        most = self.steps + self.layers - 1
        self.pad = round_up(most - 1, 8)
        self.width = round_up(self.strip + 2 * self.pad, 16)
        self.edge = round_up(most + 8, 16)
        self.total = self.rows_n * self.width
        self.first = min(FIRST, self.steps)
        needs = [most, most - 1] + [most - step for step in range(self.steps)]
        split = 2 + self.first
        self.early, self.early_rows = self.pieces(needs[:split])
        self.late, self.late_rows = self.pieces(needs[split:])

    def pieces(self, needs):
        found, begin = [], 0
        for need in needs:
            found.append(Piece(self.strip, need, begin, self.band))
            begin = found[-1].end
        return found, begin


def edge_kernel(plan, hidden_in, cell_in, maps_in, out, hidden, cell, maps, sems):
    edge, columns = plan.edge, plan.columns
    copies = [
        pltpu.make_async_copy(hidden_in, hidden, sems.at[0]),
        pltpu.make_async_copy(cell_in, cell, sems.at[1]),
        pltpu.make_async_copy(maps_in, maps, sems.at[2]),
    ]
    for copy in copies:
        copy.start()
    for copy in copies:
        copy.wait()

    def take(begin):
        out[0] = hidden[0, :, begin : begin + edge]
        out[1] = cell[0, :, begin : begin + edge].astype(BF)
        for step in range(plan.steps):
            out[2 + step] = maps[step, :, begin : begin + edge]

    @pl.when(lax.axis_index("cols") == 0)
    def _():
        take(columns - edge)

    @pl.when(lax.axis_index("cols") != 0)
    def _():
        take(0)


def pack_kernel(plan, pieces, at_edge, hidden, cell, maps, left, right, *refs):
    outs, padded = refs[-1 - plan.count : -1], refs[-1]
    edge, columns, chans, band = plan.edge, plan.columns, plan.chans, plan.band
    place, col = lax.axis_index("rows"), lax.axis_index("cols")
    for number, piece in enumerate(pieces):
        source = at_edge + number
        if source == 0:
            whole = hidden[0]
        elif source == 1:
            whole = cell[0]
        else:
            whole = maps[source - 2]
        before = jnp.where(col > 0, left[source].astype(F32), 0.0)
        after = jnp.where(col < plan.cols - 1, right[source].astype(F32), 0.0)
        padded[number, :, 0:edge] = before
        padded[number, :, edge : edge + columns] = whole.astype(F32)
        padded[number, :, edge + columns : 2 * edge + columns] = after
    for hop in range(plan.count):
        target = partner(place, hop, plan.count)[0]
        for number, piece in enumerate(pieces):
            inset = edge - piece.left
            rest = inset % 8
            start = pl.multiple_of(target * plan.strip + (inset - rest), 8)
            loaded = piece.extent + (8 if rest else 0)
            value = padded[number, :, pl.ds(start, loaded), :]
            if rest:
                value = value.reshape(band * loaded, chans)
                value = pltpu.roll(value, band * loaded - rest, 0)
                value = value.reshape(band, loaded, chans)[:, : piece.extent]
            value = value.reshape(band * piece.extent, chans)
            outs[hop][piece.begin : piece.end] = value.astype(BF)


def takes_early(plan, phase, first_step):
    return first_step == 0 or (phase == 0 and first_step < plan.first)


def takes_late(plan, phase, last_step):
    return phase == 0 and last_step > plan.first


def chunk_kernel(plan, phase, first_step, last_step, *refs):
    refs = list(refs)
    rows_n, band, width, chans = plan.rows_n, plan.band, plan.width, plan.chans
    count, total, steps = plan.count, plan.total, plan.steps
    early = late = None
    if takes_early(plan, phase, first_step):
        early = [refs.pop(0) for _ in range(count)]
    if takes_late(plan, phase, last_step):
        late = [refs.pop(0) for _ in range(count)]
    maps_ref = None if phase == 0 else refs.pop(0)
    hidden_ref = cell_ref = None
    if first_step > 0:
        hidden_ref, cell_ref = refs.pop(0), refs.pop(0)
    weights, bias, _ = refs[:3]
    hidden_out, cell_out, kept, slab = refs[3:]

    @pl.when(lax.axis_index("pipe") == phase)
    def _():
        place = lax.axis_index("rows")
        sources = [partner(place, hop, count)[1] for hop in range(count)]
        start_column = (
            lax.axis_index("cols") * plan.columns + place * plan.strip - plan.pad
        )
        blank = jnp.zeros((width, 6 * chans), BF)
        slab[0:width, :] = blank
        slab[total + width : total + 2 * width, :] = blank

        def spread(lane, value):
            value = value.astype(F32)
            for tap in range(3):
                moved = value if tap == 1 else pltpu.roll(value, (1 - tap) % total, 0)
                at = 2 * chans * tap + lane
                slab[width : width + total, at : at + chans] = moved.astype(BF)

        def bands(lane, refs_in, piece):
            for hop in range(count):
                flat = refs_in[hop][piece.begin : piece.end].astype(F32)
                extent = piece.extent
                if extent < width:
                    flat = flat.reshape(band, extent, chans)
                    fill = jnp.zeros((band, width - extent, chans), F32)
                    flat = jnp.concatenate([flat, fill], axis=1).reshape(band * width, chans)
                    extent = width
                source = sources[hop]
                for tap in range(3) if lane is not None else (1,):
                    shift = (plan.pad - piece.left + 1 - tap) % (band * extent)
                    moved = pltpu.roll(flat, shift, 0) if shift else flat
                    moved = moved.reshape(band, extent, chans)[:, :width]
                    moved = moved.reshape(band * width, chans)
                    if lane is None:
                        start = pl.multiple_of(source * band * width, 16)
                        cell_out[pl.ds(start, band * width), :] = moved
                    else:
                        at = 2 * chans * tap + lane
                        start = pl.multiple_of((source * band + 1) * width, 16)
                        slab[pl.ds(start, band * width), at : at + chans] = moved.astype(BF)

        hidden = None
        cell = None
        for step in range(first_step, last_step):
            if step == 0:
                bands(chans, early, plan.early[0])
                bands(None, early, plan.early[1])
                cell = cell_out[...]
            elif step == first_step:
                spread(chans, hidden_ref[hidden_ref.shape[0] - 1].reshape(total, chans))
                cell = cell_ref[...]
            else:
                spread(chans, hidden.reshape(total, chans))
            if phase > 0:
                spread(0, maps_ref[step - first_step].reshape(total, chans))
            elif step < plan.first:
                bands(0, early, plan.early[2 + step])
            else:
                bands(0, late, plan.late[step - plan.first])

            depth = 6 * chans
            gates = bias[...]
            for tap in range(3):
                gates = gates + jnp.dot(
                    slab[tap * width : tap * width + total, :],
                    weights[tap * depth : (tap + 1) * depth, :],
                    preferred_element_type=F32,
                )
            cell = sigmoid(gates[:, chans : 2 * chans]) * cell + sigmoid(
                gates[:, :chans]
            ) * jnp.tanh(gates[:, 2 * chans : 3 * chans])
            hidden = sigmoid(gates[:, 3 * chans :]) * jnp.tanh(cell)
            hidden = hidden.reshape(rows_n, width, chans)
            column = start_column + lax.broadcasted_iota(jnp.int32, hidden.shape, 1)
            inside = jnp.logical_and(column >= 0, column < plan.grid_columns)
            hidden = jnp.where(inside, hidden, 0.0).astype(BF)
            hidden_out[step - first_step] = hidden
            kept[:, step] = hidden
        cell_out[...] = cell
        if last_step == steps:
            kept[:, steps] = cell.astype(BF).reshape(rows_n, width, chans)


def advance(plan, phase, first_step, last_step, feed, kept):
    vmem = pl.BlockSpec(memory_space=pltpu.VMEM)
    operands = [*feed, kept]
    chunk = last_step - first_step
    return pl.pallas_call(
        functools.partial(chunk_kernel, plan, phase, first_step, last_step),
        out_shape=(
            jax.ShapeDtypeStruct((chunk, plan.rows_n, plan.width, plan.chans), BF),
            jax.ShapeDtypeStruct((plan.total, plan.chans), F32),
            jax.ShapeDtypeStruct(kept.shape, kept.dtype),
        ),
        in_specs=[vmem] * len(operands),
        out_specs=(vmem, vmem, vmem),
        scratch_shapes=[pltpu.VMEM((plan.total + 2 * plan.width, 6 * plan.chans), BF)],
        input_output_aliases={len(operands) - 1: 2},
        compiler_params=pltpu.CompilerParams(vmem_limit_bytes=VMEM_LIMIT),
        cost_estimate=pl.CostEstimate(
            flops=2 * chunk * plan.total * 18 * plan.chans * 4 * plan.chans,
            bytes_accessed=1000000,
            transcendentals=5 * chunk * plan.total * plan.chans,
        ),
    )(*operands)


def pack(plan, pieces, rows, at_edge, arrays, after=()):
    vmem = pl.BlockSpec(memory_space=pltpu.VMEM)
    shape = (len(pieces), plan.band, plan.columns + 2 * plan.edge, plan.chans)
    return pl.pallas_call(
        functools.partial(pack_kernel, plan, pieces, at_edge),
        out_shape=(jax.ShapeDtypeStruct((rows, plan.chans), BF),) * plan.count,
        in_specs=[vmem] * len(arrays) + [pl.BlockSpec(memory_space=pl.ANY)] * len(after),
        out_specs=(vmem,) * plan.count,
        scratch_shapes=[pltpu.VMEM(shape, F32)],
        compiler_params=pltpu.CompilerParams(vmem_limit_bytes=VMEM_LIMIT),
    )(*arrays, *after)


def exchange(plan, pieces):
    got = [pieces[0]]
    for hop in range(1, plan.count):
        route = [(n, partner(n, hop, plan.count)[0]) for n in range(plan.count)]
        got.append(lax.ppermute(pieces[hop], "rows", route))
    return got


def shards(inputs, hidden_init, cell_init, kernels, biases):
    plan = Plan(inputs)
    place = lax.axis_index("rows")
    steps, band, chans, count, layers = (
        plan.steps,
        plan.band,
        plan.chans,
        plan.count,
        plan.layers,
    )
    weights, bias = kernels[0], biases

    if plan.cols == 2:
        vmem = pl.BlockSpec(memory_space=pltpu.VMEM)
        anywhere = pl.BlockSpec(memory_space=pl.ANY)
        sources = (hidden_init, cell_init, inputs)
        beside, *sources = pl.pallas_call(
            functools.partial(edge_kernel, plan),
            out_shape=[jax.ShapeDtypeStruct((2 + steps, band, plan.edge, chans), BF)]
            + [jax.ShapeDtypeStruct(source.shape, source.dtype) for source in sources],
            in_specs=[anywhere] * 3,
            out_specs=[vmem] * 4,
            scratch_shapes=[pltpu.SemaphoreType.DMA((3,))],
            compiler_params=pltpu.CompilerParams(vmem_limit_bytes=VMEM_LIMIT),
        )(*sources)
        left = right = lax.ppermute(beside, "cols", [(0, 1), (1, 0)])
    else:
        sources = (hidden_init, cell_init, inputs)
        maps = jnp.concatenate([hidden_init, cell_init.astype(BF), inputs], axis=0)
        ring = [(n, (n + 1) % plan.cols) for n in range(plan.cols)]
        left = lax.ppermute(maps[:, :, plan.columns - plan.edge :], "cols", ring)
        right = lax.ppermute(maps[:, :, : plan.edge], "cols", [(b, a) for a, b in ring])
    arrays = [*sources, left, right]
    early_pieces = pack(plan, plan.early, plan.early_rows, 0, arrays)
    early = exchange(plan, early_pieces)
    late_pieces = pack(
        plan, plan.late, plan.late_rows, len(plan.early), arrays, early_pieces[:1]
    )
    late = exchange(plan, late_pieces)

    kept = jnp.zeros((plan.rows_n, steps + 1, plan.width, chans), BF)
    chunks = [(first, min(first + CHUNK, steps)) for first in range(0, steps, CHUNK)]
    order = sorted(
        (number + LAG * phase, -phase, number)
        for phase in range(layers)
        for number in range(len(chunks))
    )
    state = [[] for _ in range(layers)]
    sent = {}
    for _, minus_phase, number in order:
        phase = -minus_phase
        first_step, last_step = chunks[number]
        feed = list(early) if takes_early(plan, phase, first_step) else []
        feed += late if takes_late(plan, phase, last_step) else []
        feed += [sent[phase - 1, number]] if phase > 0 else []
        feed += state[phase]
        hidden, cell, kept = advance(
            plan, phase, first_step, last_step, feed + [weights, bias], kept
        )
        state[phase] = [hidden, cell]
        if phase < layers - 1:
            ring = [(n, (n + 1) % layers) for n in range(layers)]
            sent[phase, number] = lax.ppermute(hidden, "pipe", ring)

    def out_piece(hop):
        target = partner(place, hop, count)[0]
        piece = lax.dynamic_slice_in_dim(kept, target * band, band, axis=0)
        return piece[:, :, plan.pad : plan.pad + plan.strip]

    out = jnp.zeros((band, steps + 1, plan.columns, chans), BF)
    for hop, piece in enumerate(exchange(plan, [out_piece(hop) for hop in range(count)])):
        source = partner(place, hop, count)[1]
        out = lax.dynamic_update_slice_in_dim(out, piece, source * plan.strip, axis=2)
    produced = jnp.swapaxes(out[:, :steps], 0, 1)
    final = out[:, steps].astype(F32)
    return produced[None], final[None]


def solution(mesh):
    return jax.shard_map(
        shards,
        mesh=mesh,
        in_specs=(
            P(None, ("groups", "rows"), "cols", None),
            P("pipe", ("groups", "rows"), "cols", None),
            P("pipe", ("groups", "rows"), "cols", None),
            P("pipe", None, None),
            P("pipe", None),
        ),
        out_specs=(
            P("pipe", None, ("groups", "rows"), "cols", None),
            P("pipe", ("groups", "rows"), "cols", None),
        ),
        check_vma=False,
    )
```

```python
import functools

import jax
import jax.numpy as jnp
from jax import lax
from jax.experimental import pallas as pl
from jax.experimental.pallas import tpu as pltpu
from jax.sharding import PartitionSpec as P

BF = jnp.bfloat16
F32 = jnp.float32
CHUNKS = (2, 2, 2, 2)
LAG = 3
FIRST = 2
LENT = 4
EARLY_OUT = 4
LEND_AFTER = False
SPREAD = True
MIB = 1024 * 1024


def round_up(value, unit):
    return -(-value // unit) * unit


def partner(index, hop, count):
    if count & (count - 1) == 0:
        return index ^ hop, index ^ hop
    return (index + hop) % count, (index + count - hop) % count


def hop_at(number, count):
    if not SPREAD or number == 0:
        return number
    return jnp.where(lax.axis_index("cols") % 2 == 0, number, count - number)


def sigmoid(value):
    return 0.5 * jnp.tanh(0.5 * value) + 0.5


class Piece:
    def __init__(self, strip, need, begin, band):
        self.extent = round_up(strip + 2 * need, 8)
        self.left = (self.extent - strip) // 2
        self.begin = begin
        self.end = begin + band * self.extent


class Plan:
    def __init__(self, inputs):
        self.steps, self.band, self.columns, self.chans = inputs.shape
        self.count = lax.axis_size("rows")
        self.cols = lax.axis_size("cols")
        self.layers = lax.axis_size("pipe")
        self.grid_columns = self.columns * self.cols
        self.rows_n = self.band * self.count
        self.strip = self.columns // self.count
        most = self.steps + self.layers - 1
        self.pad = round_up(most - 1, 8)
        self.width = round_up(self.strip + 2 * self.pad, 16)
        self.total = self.rows_n * self.width
        self.room = 4 * MIB + self.total * self.chans * (4 * 4 * 6 + 12)
        self.lent_steps = min(LENT, self.steps - 1) if self.layers > 1 else 0
        own = self.steps - self.lent_steps
        self.first = min(FIRST, own)
        needs = [most, most - 1] + [most - step for step in range(self.steps)]
        inputs_of = lambda begin, end: [2 + step for step in range(begin, end)]
        self.early, rows_a = self.pieces(needs, [0, 1] + inputs_of(0, self.first))
        self.late, rows_b = self.pieces(needs, inputs_of(self.first, own))
        self.lent, self.lent_rows = self.pieces(needs, inputs_of(own, self.steps))
        self.state, rows_c = self.pieces(needs, [0, 1])
        self.early_rows = max(rows_a, self.lent_rows)
        self.late_rows = max(rows_b, rows_c)
        half = min(EARLY_OUT, self.steps)
        self.bounds = [(0, half), (half, self.steps + 1)]
        self.edge = round_up(max((self.pieces(needs, [n])[0][n].left for n in range(len(needs)))) + 4, 16)

    def reach(self, phase, step):
        return (self.steps - 1 - step) + (self.layers - 1 - phase)

    def lends(self, phase, first_step):
        return LEND_AFTER and self.lent_steps > 0 and phase == 0 and first_step == 0

    def extent(self, phase, first_step, last_step):
        return min(round_up(self.strip + 2 * self.reach(phase, first_step), 8), self.width)

    def pieces(self, needs, numbers):
        found, begin = {}, 0
        for number in numbers:
            found[number] = Piece(self.strip, needs[number], begin, self.band)
            begin = found[number].end
        return found, begin


def edge_kernel(plan, maps, out):
    edge, columns = plan.edge, plan.columns

    @pl.when(lax.axis_index("cols") == 0)
    def _():
        out[...] = maps[:, :, columns - edge :]

    @pl.when(lax.axis_index("cols") != 0)
    def _():
        out[...] = maps[:, :, :edge]


def pack_kernel(plan, maps, left, right, *refs):
    early, late, padded = refs[: plan.count], refs[plan.count : -1], refs[-1]
    edge, columns, chans, band = plan.edge, plan.columns, plan.chans, plan.band
    place, col = lax.axis_index("rows"), lax.axis_index("cols")

    def fill(groups):
        for outs, pieces in groups:
            for number, piece in pieces.items():
                before = jnp.where(col > 0, left[number].astype(F32), 0.0)
                after = jnp.where(col < plan.cols - 1, right[number].astype(F32), 0.0)
                padded[number, :, 0:edge] = before
                padded[number, :, edge : edge + columns] = maps[number].astype(F32)
                padded[number, :, edge + columns : 2 * edge + columns] = after
        for outs, pieces in groups:
            for number, piece in pieces.items():
                for hop in range(plan.count):
                    target = partner(place, hop_at(hop, plan.count), plan.count)[0]
                    inset = edge - piece.left
                    rest = inset % 8
                    start = pl.multiple_of(target * plan.strip + (inset - rest), 8)
                    loaded = piece.extent + (8 if rest else 0)
                    value = padded[number, :, pl.ds(start, loaded), :]
                    if rest:
                        value = value.reshape(band * loaded, chans)
                        value = pltpu.roll(value, band * loaded - rest, 0)
                        value = value.reshape(band, loaded, chans)[:, : piece.extent]
                    value = value.reshape(band * piece.extent, chans)
                    outs[hop][piece.begin : piece.end] = value.astype(BF)

    @pl.when(lax.axis_index("pipe") == 0)
    def _():
        fill([(early, plan.early), (late, plan.late)])

    @pl.when(lax.axis_index("pipe") != 0)
    def _():
        fill([(early, plan.lent), (late, plan.state)])


def needed(plan, phase, first_step, last_step):
    if phase > 0:
        return [False, first_step == 0, False]
    own = plan.steps - plan.lent_steps
    return [
        first_step < plan.first,
        first_step < own and last_step > plan.first,
        last_step > own,
    ]


def chunk_kernel(plan, phase, first_step, last_step, parts, *refs):
    refs = list(refs)
    rows_n, band, width, chans = plan.rows_n, plan.band, plan.width, plan.chans
    count, total, steps = plan.count, plan.total, plan.steps
    early, late, lent = needed(plan, phase, first_step, last_step)
    early = [(refs.pop(0), 0) for _ in range(count)] if early else None
    late = [(refs.pop(0), 0) for _ in range(count)] if late else None
    if lent:
        lender = refs.pop(0)
        lent = [(lender, hop * plan.lent_rows) for hop in range(count)]
    maps_ref = None if phase == 0 else refs.pop(0)
    hidden_ref = cell_ref = None
    if first_step > 0:
        hidden_ref, cell_ref = refs.pop(0), refs.pop(0)
    weights, bias = refs[:2]
    outs, (slab, fresh) = refs[2 + parts : -2], refs[-2:]
    outs, kept = list(outs[:-parts]), outs[-parts:]
    hidden_out = outs.pop(0) if last_step < steps or phase < plan.layers - 1 else None
    cell_out = outs.pop(0) if last_step < steps else None
    if plan.lends(phase, first_step):
        borrowed = outs.pop(0)

        @pl.when(lax.axis_index("pipe") != phase)
        def _():
            for hop in range(count):
                begin = hop * plan.lent_rows
                borrowed[begin : begin + plan.lent_rows] = early[hop][0][: plan.lent_rows]

    bounds = plan.bounds[-len(kept) :]

    def keep(at, value):
        for ref, (begin, end) in zip(kept, bounds):
            if begin <= at < end:
                ref[:, at - begin] = value

    @pl.when(lax.axis_index("pipe") == phase)
    def _():
        place = lax.axis_index("rows")
        sources = [partner(place, hop_at(hop, count), count)[1] for hop in range(count)]
        start_column = (
            lax.axis_index("cols") * plan.columns + place * plan.strip - plan.pad
        )
        blank = jnp.zeros((width, 6 * chans), BF)
        slab[0:width, :] = blank
        slab[total + width : total + 2 * width, :] = blank

        def spread(lane, value):
            value = value.astype(F32)
            extent = value.shape[1]
            left = plan.pad if extent == width else (extent - plan.strip) // 2
            if extent < width:
                fill = jnp.zeros((rows_n, width - extent, chans), F32)
                value = jnp.concatenate([value, fill], axis=1)
            value = value.reshape(total, chans)
            for tap in range(3):
                shift = (plan.pad - left + 1 - tap) % total
                moved = pltpu.roll(value, shift, 0) if shift else value
                at = 2 * chans * tap + lane
                slab[width : width + total, at : at + chans] = moved.astype(BF)

        def bands(lane, refs_in, piece):
            for hop in range(count):
                ref, offset = refs_in[hop]
                flat = ref[offset + piece.begin : offset + piece.end].astype(F32)
                extent = piece.extent
                if extent < width:
                    flat = flat.reshape(band, extent, chans)
                    fill = jnp.zeros((band, width - extent, chans), F32)
                    flat = jnp.concatenate([flat, fill], axis=1).reshape(band * width, chans)
                    extent = width
                source = sources[hop]
                for tap in range(3) if lane is not None else (1,):
                    shift = (plan.pad - piece.left + 1 - tap) % (band * extent)
                    moved = pltpu.roll(flat, shift, 0) if shift else flat
                    moved = moved.reshape(band, extent, chans)[:, :width]
                    moved = moved.reshape(band * width, chans)
                    if lane is None:
                        start = pl.multiple_of(source * band * width, 16)
                        fresh[pl.ds(start, band * width), :] = moved
                    else:
                        at = 2 * chans * tap + lane
                        start = pl.multiple_of((source * band + 1) * width, 16)
                        slab[pl.ds(start, band * width), at : at + chans] = moved.astype(BF)

        hidden = None
        cell = None
        for step in range(first_step, last_step):
            if step == 0:
                pieces, from_refs = (plan.state, late) if phase > 0 else (plan.early, early)
                bands(chans, from_refs, pieces[0])
                bands(None, from_refs, pieces[1])
                cell = fresh[...]
            elif step == first_step:
                spread(chans, hidden_ref[hidden_ref.shape[0] - 1])
                cell = cell_ref[...]
            else:
                spread(chans, hidden)
            if phase > 0:
                spread(0, maps_ref[step - first_step])
            elif step < plan.first:
                bands(0, early, plan.early[2 + step])
            elif step < steps - plan.lent_steps:
                bands(0, late, plan.late[2 + step])
            else:
                bands(0, lent, plan.lent[2 + step])

            depth = 6 * chans
            gates = bias[0:1]
            for tap in range(3):
                gates = gates + jnp.dot(
                    slab[tap * width : tap * width + total, :],
                    weights[tap * depth : (tap + 1) * depth, :],
                    preferred_element_type=F32,
                )
            cell = sigmoid(gates[:, chans : 2 * chans]) * cell + sigmoid(
                gates[:, :chans]
            ) * jnp.tanh(gates[:, 2 * chans : 3 * chans])
            hidden = sigmoid(gates[:, 3 * chans :]) * jnp.tanh(cell)
            hidden = hidden.reshape(rows_n, width, chans)
            column = start_column + lax.broadcasted_iota(jnp.int32, hidden.shape, 1)
            inside = jnp.logical_and(column >= 0, column < plan.grid_columns)
            hidden = jnp.where(inside, hidden, 0.0)
            extent = hidden_out.shape[2] if hidden_out is not None else width
            if extent < width:
                shift = plan.pad - (extent - plan.strip) // 2
                moved = pltpu.roll(hidden.reshape(total, chans), total - shift, 0)
                moved = moved.reshape(rows_n, width, chans)[:, :extent]
                hidden_out[step - first_step] = moved.astype(BF)
            elif hidden_out is not None:
                hidden_out[step - first_step] = hidden.astype(BF)
            hidden = hidden.astype(BF)
            keep(step, hidden)
        if cell_out is not None:
            cell_out[...] = cell
        if last_step == steps:
            keep(steps, cell.astype(BF).reshape(rows_n, width, chans))


def advance(plan, phase, first_step, last_step, feed, kept):
    vmem = pl.BlockSpec(memory_space=pltpu.VMEM)
    operands = [*feed, *kept]
    chunk = last_step - first_step
    extent = plan.extent(phase, first_step, last_step)
    outs = []
    if last_step < plan.steps or phase < plan.layers - 1:
        outs.append(jax.ShapeDtypeStruct((chunk, plan.rows_n, extent, plan.chans), BF))
    if last_step < plan.steps:
        outs.append(jax.ShapeDtypeStruct((plan.total, plan.chans), F32))
    if plan.lends(phase, first_step):
        outs.append(jax.ShapeDtypeStruct((plan.count * plan.lent_rows, plan.chans), BF))
    aliases = {len(feed) + n: len(outs) + n for n in range(len(kept))}
    outs += [jax.ShapeDtypeStruct(part.shape, part.dtype) for part in kept]
    return pl.pallas_call(
        functools.partial(chunk_kernel, plan, phase, first_step, last_step, len(kept)),
        out_shape=outs,
        in_specs=[vmem] * len(operands),
        out_specs=[vmem] * len(outs),
        scratch_shapes=[
            pltpu.VMEM((plan.total + 2 * plan.width, 6 * plan.chans), BF),
            pltpu.VMEM((plan.total, plan.chans), F32),
        ],
        input_output_aliases=aliases,
        compiler_params=pltpu.CompilerParams(vmem_limit_bytes=plan.room),
        cost_estimate=pl.CostEstimate(
            flops=2 * chunk * plan.total * 18 * plan.chans * 4 * plan.chans,
            bytes_accessed=1000000,
            transcendentals=5 * chunk * plan.total * plan.chans,
        ),
    )(*operands)


def merge_kernel(plan, *refs):
    maps_out, cell_out = refs[-2:]
    place = lax.axis_index("rows")
    for hop in range(plan.count):
        source = partner(place, hop_at(hop, plan.count), plan.count)[1]
        columns = pl.ds(pl.multiple_of(source * plan.strip, plan.strip), plan.strip)
        for number, (begin, end) in enumerate(plan.bounds):
            part = refs[number * plan.count + hop]
            for step in range(begin, min(end, plan.steps)):
                maps_out[0, step, :, columns, :] = part[:, step - begin]
            if end > plan.steps:
                cell_out[0, :, columns, :] = part[:, plan.steps - begin].astype(F32)


def pack(plan, arrays):
    vmem = pl.BlockSpec(memory_space=pltpu.VMEM)
    shape = (2 + plan.steps, plan.band, plan.columns + 2 * plan.edge, plan.chans)
    rows = [plan.early_rows] * plan.count + [plan.late_rows] * plan.count
    return pl.pallas_call(
        functools.partial(pack_kernel, plan),
        out_shape=[jax.ShapeDtypeStruct((extent, plan.chans), BF) for extent in rows],
        in_specs=[vmem] * len(arrays),
        out_specs=[vmem] * len(rows),
        scratch_shapes=[pltpu.VMEM(shape, F32)],
        compiler_params=pltpu.CompilerParams(vmem_limit_bytes=plan.room),
    )(*arrays)


def load_kernel(weights_in, bias_in, _, weights, bias, sems):
    copies = [
        pltpu.make_async_copy(weights_in, weights, sems.at[0]),
        pltpu.make_async_copy(bias_in, bias, sems.at[1]),
    ]
    for copy in copies:
        copy.start()
    for copy in copies:
        copy.wait()


def settle(plan, parts, kept):
    vmem = pl.BlockSpec(memory_space=pltpu.VMEM)
    return pl.pallas_call(
        lambda *refs: None,
        out_shape=jax.ShapeDtypeStruct(kept.shape, kept.dtype),
        in_specs=[vmem] * (1 + len(parts)),
        out_specs=vmem,
        input_output_aliases={len(parts): 0},
        compiler_params=pltpu.CompilerParams(vmem_limit_bytes=plan.room),
    )(*parts, kept)


def exchange(plan, pieces):
    got = [pieces[0]]
    for number in range(1, plan.count):
        route = []
        for row in range(plan.count):
            for col in range(plan.cols):
                hop = plan.count - number if SPREAD and col % 2 else number
                target = partner(row, hop, plan.count)[0]
                route.append((row * plan.cols + col, target * plan.cols + col))
        got.append(lax.ppermute(pieces[number], ("rows", "cols"), route))
    return got


def shards(inputs, hidden_init, cell_init, kernels, biases):
    plan = Plan(inputs)
    place = lax.axis_index("rows")
    steps, band, chans, count, layers = (
        plan.steps,
        plan.band,
        plan.chans,
        plan.count,
        plan.layers,
    )
    vmem = pl.BlockSpec(memory_space=pltpu.VMEM)
    params = pltpu.CompilerParams(vmem_limit_bytes=plan.room)
    maps = jnp.concatenate([hidden_init, cell_init.astype(BF), inputs], axis=0)
    if plan.cols == 2:
        beside = pl.pallas_call(
            functools.partial(edge_kernel, plan),
            out_shape=jax.ShapeDtypeStruct((2 + steps, band, plan.edge, chans), BF),
            in_specs=[vmem],
            out_specs=vmem,
            compiler_params=params,
        )(maps)
        left = right = lax.ppermute(beside, "cols", [(0, 1), (1, 0)])
    else:
        ring = [(n, (n + 1) % plan.cols) for n in range(plan.cols)]
        left = lax.ppermute(maps[:, :, plan.columns - plan.edge :], "cols", ring)
        right = lax.ppermute(maps[:, :, : plan.edge], "cols", [(b, a) for a, b in ring])
    packed = pack(plan, [maps, left, right])
    weights, bias = pl.pallas_call(
        load_kernel,
        out_shape=[jax.ShapeDtypeStruct(part.shape, part.dtype) for part in (kernels[0], biases)],
        in_specs=[pl.BlockSpec(memory_space=pltpu.HBM)] * 2 + [vmem],
        out_specs=[vmem] * 2,
        scratch_shapes=[pltpu.SemaphoreType.DMA((2,))],
        compiler_params=params,
    )(kernels[0], biases, packed[0])
    early = exchange(plan, packed[:count])
    late = exchange(plan, packed[count:])
    lent = []
    back = [(n, (n - 1) % layers) for n in range(layers)]
    if plan.lent_steps and not LEND_AFTER:
        borrowed = jnp.concatenate([piece[: plan.lent_rows] for piece in early], axis=0)
        lent = [lax.ppermute(borrowed, "pipe", back)]

    kept = [
        jnp.zeros((plan.rows_n, end - begin, plan.width, chans), BF) for begin, end in plan.bounds
    ]

    def out_piece(part, hop):
        target = partner(place, hop_at(hop, count), count)[0]
        piece = lax.dynamic_slice_in_dim(part, target * band, band, axis=0)
        return piece[:, :, plan.pad : plan.pad + plan.strip]

    chunks = []
    while not chunks or chunks[-1][1] < steps:
        begin = chunks[-1][1] if chunks else 0
        size = CHUNKS[len(chunks)] if len(chunks) < len(CHUNKS) else 1
        chunks.append((begin, min(begin + size, steps)))
    order = sorted(
        (number + LAG * phase, -phase, number)
        for phase in range(layers)
        for number in range(len(chunks))
    )
    state = [[] for _ in range(layers)]
    sent = {}
    parts = []
    for _, minus_phase, number in order:
        phase = -minus_phase
        first_step, last_step = chunks[number]
        takes = needed(plan, phase, first_step, last_step)
        feed = []
        for wanted, arrays in zip(takes, (early, late, lent)):
            feed += arrays if wanted else []
        feed += [sent[phase - 1, number]] if phase > 0 else []
        feed += state[phase]
        results = advance(plan, phase, first_step, last_step, feed + [weights, bias], kept)
        results, kept = list(results[: -len(kept)]), list(results[-len(kept) :])
        if plan.lends(phase, first_step):
            lent = [lax.ppermute(results.pop(), "pipe", back)]
        if last_step < steps:
            state[phase] = results
        if phase < layers - 1:
            hidden = results[0]
            ring = [(n, (n + 1) % layers) for n in range(layers)]
            sent[phase, number] = lax.ppermute(hidden, "pipe", ring)
        if phase == layers - 1 and last_step >= plan.bounds[0][1] and len(kept) == 2:
            done = kept.pop(0)
            parts += exchange(plan, [out_piece(done, hop) for hop in range(count)])
    rest = settle(plan, parts[1:2], kept[0])
    parts += exchange(plan, [out_piece(rest, hop) for hop in range(count)])
    vmem = pl.BlockSpec(memory_space=pltpu.VMEM)
    return pl.pallas_call(
        functools.partial(merge_kernel, plan),
        out_shape=(
            jax.ShapeDtypeStruct((1, steps, band, plan.columns, chans), BF),
            jax.ShapeDtypeStruct((1, band, plan.columns, chans), F32),
        ),
        in_specs=[vmem] * len(parts),
        out_specs=(vmem, vmem),
        compiler_params=pltpu.CompilerParams(vmem_limit_bytes=plan.room),
    )(*parts)


def solution(mesh):
    return jax.shard_map(
        shards,
        mesh=mesh,
        in_specs=(
            P(None, ("groups", "rows"), "cols", None),
            P("pipe", ("groups", "rows"), "cols", None),
            P("pipe", ("groups", "rows"), "cols", None),
            P("pipe", None, None),
            P("pipe", None),
        ),
        out_specs=(
            P("pipe", None, ("groups", "rows"), "cols", None),
            P("pipe", ("groups", "rows"), "cols", None),
        ),
        check_vma=False,
    )
```

```python
import functools

import jax
import jax.numpy as jnp
from jax import lax
from jax.experimental import pallas as pl
from jax.experimental.pallas import tpu as pltpu
from jax.sharding import PartitionSpec as P

BF = jnp.bfloat16
F32 = jnp.float32
CHUNKS = (2, 2, 2, 2)
LAG = 3
FIRST = 2
LENT = 3
EARLY_OUT = 4
LEND_AFTER = False
SPREAD = True
LEND_ONE_WAY = True
HAND_ONE_WAY = True
MIB = 1024 * 1024


def round_up(value, unit):
    return -(-value // unit) * unit


def partner(index, hop, count):
    if count & (count - 1) == 0:
        return index ^ hop, index ^ hop
    return (index + hop) % count, (index + count - hop) % count


def hop_at(number, count):
    if not SPREAD or number == 0:
        return number
    return jnp.where(lax.axis_index("cols") % 2 == 0, number, count - number)


def sigmoid(value):
    return 0.5 * jnp.tanh(0.5 * value) + 0.5


class Piece:
    def __init__(self, strip, need, begin, band):
        self.extent = round_up(strip + 2 * need, 8)
        self.left = (self.extent - strip) // 2
        self.begin = begin
        self.end = begin + band * self.extent


class Plan:
    def __init__(self, inputs):
        self.steps, self.band, self.columns, self.chans = inputs.shape
        self.count = lax.axis_size("rows")
        self.cols = lax.axis_size("cols")
        self.layers = lax.axis_size("pipe")
        self.grid_columns = self.columns * self.cols
        self.rows_n = self.band * self.count
        self.strip = self.columns // self.count
        most = self.steps + self.layers - 1
        self.pad = round_up(most - 1, 8)
        self.width = round_up(self.strip + 2 * self.pad, 16)
        self.total = self.rows_n * self.width
        self.room = 4 * MIB + self.total * self.chans * (4 * 4 * 6 + 12)
        self.lent_steps = min(LENT, self.steps - 1) if self.layers > 1 else 0
        own = self.steps - self.lent_steps
        self.first = min(FIRST, own)
        needs = [most, most - 1] + [most - step for step in range(self.steps)]
        inputs_of = lambda begin, end: [2 + step for step in range(begin, end)]
        self.early, rows_a = self.pieces(needs, [0, 1] + inputs_of(0, self.first))
        self.late, rows_b = self.pieces(needs, inputs_of(self.first, own))
        self.lent, self.lent_rows = self.pieces(needs, inputs_of(own, self.steps))
        self.state, rows_c = self.pieces(needs, [0, 1])
        self.early_rows = max(rows_a, self.lent_rows)
        self.late_rows = max(rows_b, rows_c)
        half = min(EARLY_OUT, self.steps)
        self.bounds = [(0, half), (half, self.steps + 1)]
        self.edge = round_up(max((self.pieces(needs, [n])[0][n].left for n in range(len(needs)))) + 4, 16)

    def reach(self, phase, step):
        return (self.steps - 1 - step) + (self.layers - 1 - phase)

    def lends(self, phase, first_step):
        return LEND_AFTER and self.lent_steps > 0 and phase == 0 and first_step == 0

    def extent(self, phase, first_step, last_step):
        return min(round_up(self.strip + 2 * self.reach(phase, first_step), 8), self.width)

    def pieces(self, needs, numbers):
        found, begin = {}, 0
        for number in numbers:
            found[number] = Piece(self.strip, needs[number], begin, self.band)
            begin = found[number].end
        return found, begin


def edge_kernel(plan, maps, out):
    edge, columns = plan.edge, plan.columns

    @pl.when(lax.axis_index("cols") == 0)
    def _():
        out[...] = maps[:, :, columns - edge :]

    @pl.when(lax.axis_index("cols") != 0)
    def _():
        out[...] = maps[:, :, :edge]


def pack_kernel(plan, maps, left, right, *refs):
    early, late, padded = refs[: plan.count], refs[plan.count : -1], refs[-1]
    edge, columns, chans, band = plan.edge, plan.columns, plan.chans, plan.band
    place, col = lax.axis_index("rows"), lax.axis_index("cols")

    def fill(groups):
        for outs, pieces in groups:
            for number, piece in pieces.items():
                before = jnp.where(col > 0, left[number].astype(F32), 0.0)
                after = jnp.where(col < plan.cols - 1, right[number].astype(F32), 0.0)
                padded[number, :, 0:edge] = before
                padded[number, :, edge : edge + columns] = maps[number].astype(F32)
                padded[number, :, edge + columns : 2 * edge + columns] = after
        for outs, pieces in groups:
            for number, piece in pieces.items():
                for hop in range(plan.count):
                    target = partner(place, hop_at(hop, plan.count), plan.count)[0]
                    inset = edge - piece.left
                    rest = inset % 8
                    start = pl.multiple_of(target * plan.strip + (inset - rest), 8)
                    loaded = piece.extent + (8 if rest else 0)
                    value = padded[number, :, pl.ds(start, loaded), :]
                    if rest:
                        value = value.reshape(band * loaded, chans)
                        value = pltpu.roll(value, band * loaded - rest, 0)
                        value = value.reshape(band, loaded, chans)[:, : piece.extent]
                    value = value.reshape(band * piece.extent, chans)
                    outs[hop][piece.begin : piece.end] = value.astype(BF)

    @pl.when(lax.axis_index("pipe") == 0)
    def _():
        fill([(early, plan.early), (late, plan.late)])

    @pl.when(lax.axis_index("pipe") != 0)
    def _():
        fill([(early, plan.lent), (late, plan.state)])


def needed(plan, phase, first_step, last_step):
    if phase > 0:
        return [False, first_step == 0, False]
    own = plan.steps - plan.lent_steps
    return [
        first_step < plan.first,
        first_step < own and last_step > plan.first,
        last_step > own,
    ]


def chunk_kernel(plan, phase, first_step, last_step, parts, *refs):
    refs = list(refs)
    rows_n, band, width, chans = plan.rows_n, plan.band, plan.width, plan.chans
    count, total, steps = plan.count, plan.total, plan.steps
    early, late, lent = needed(plan, phase, first_step, last_step)
    early = [(refs.pop(0), 0) for _ in range(count)] if early else None
    late = [(refs.pop(0), 0) for _ in range(count)] if late else None
    if lent:
        lender = refs.pop(0)
        lent = [(lender, hop * plan.lent_rows) for hop in range(count)]
    maps_ref = None if phase == 0 else refs.pop(0)
    hidden_ref = cell_ref = None
    if first_step > 0:
        hidden_ref, cell_ref = refs.pop(0), refs.pop(0)
    weights, bias = refs[:2]
    outs, (slab, fresh) = refs[2 + parts : -2], refs[-2:]
    outs, kept = list(outs[:-parts]), outs[-parts:]
    hidden_out = outs.pop(0) if last_step < steps or phase < plan.layers - 1 else None
    cell_out = outs.pop(0) if last_step < steps else None
    if plan.lends(phase, first_step):
        borrowed = outs.pop(0)

        @pl.when(lax.axis_index("pipe") != phase)
        def _():
            for hop in range(count):
                begin = hop * plan.lent_rows
                borrowed[begin : begin + plan.lent_rows] = early[hop][0][: plan.lent_rows]

    bounds = plan.bounds[-len(kept) :]

    def keep(at, value):
        for ref, (begin, end) in zip(kept, bounds):
            if begin <= at < end:
                ref[:, at - begin] = value

    @pl.when(lax.axis_index("pipe") == phase)
    def _():
        place = lax.axis_index("rows")
        sources = [partner(place, hop_at(hop, count), count)[1] for hop in range(count)]
        start_column = (
            lax.axis_index("cols") * plan.columns + place * plan.strip - plan.pad
        )
        blank = jnp.zeros((width, 6 * chans), BF)
        slab[0:width, :] = blank
        slab[total + width : total + 2 * width, :] = blank

        def spread(lane, value):
            value = value.astype(F32)
            extent = value.shape[1]
            left = plan.pad if extent == width else (extent - plan.strip) // 2
            if extent < width:
                fill = jnp.zeros((rows_n, width - extent, chans), F32)
                value = jnp.concatenate([value, fill], axis=1)
            value = value.reshape(total, chans)
            for tap in range(3):
                shift = (plan.pad - left + 1 - tap) % total
                moved = pltpu.roll(value, shift, 0) if shift else value
                at = 2 * chans * tap + lane
                slab[width : width + total, at : at + chans] = moved.astype(BF)

        def bands(lane, refs_in, piece):
            for hop in range(count):
                ref, offset = refs_in[hop]
                flat = ref[offset + piece.begin : offset + piece.end].astype(F32)
                extent = piece.extent
                if extent < width:
                    flat = flat.reshape(band, extent, chans)
                    fill = jnp.zeros((band, width - extent, chans), F32)
                    flat = jnp.concatenate([flat, fill], axis=1).reshape(band * width, chans)
                    extent = width
                source = sources[hop]
                for tap in range(3) if lane is not None else (1,):
                    shift = (plan.pad - piece.left + 1 - tap) % (band * extent)
                    moved = pltpu.roll(flat, shift, 0) if shift else flat
                    moved = moved.reshape(band, extent, chans)[:, :width]
                    moved = moved.reshape(band * width, chans)
                    if lane is None:
                        start = pl.multiple_of(source * band * width, 16)
                        fresh[pl.ds(start, band * width), :] = moved
                    else:
                        at = 2 * chans * tap + lane
                        start = pl.multiple_of((source * band + 1) * width, 16)
                        slab[pl.ds(start, band * width), at : at + chans] = moved.astype(BF)

        hidden = None
        cell = None
        for step in range(first_step, last_step):
            if step == 0:
                pieces, from_refs = (plan.state, late) if phase > 0 else (plan.early, early)
                bands(chans, from_refs, pieces[0])
                bands(None, from_refs, pieces[1])
                cell = fresh[...]
            elif step == first_step:
                spread(chans, hidden_ref[hidden_ref.shape[0] - 1])
                cell = cell_ref[...]
            else:
                spread(chans, hidden)
            if phase > 0:
                spread(0, maps_ref[step - first_step])
            elif step < plan.first:
                bands(0, early, plan.early[2 + step])
            elif step < steps - plan.lent_steps:
                bands(0, late, plan.late[2 + step])
            else:
                bands(0, lent, plan.lent[2 + step])

            depth = 6 * chans
            gates = bias[0:1]
            for tap in range(3):
                gates = gates + jnp.dot(
                    slab[tap * width : tap * width + total, :],
                    weights[tap * depth : (tap + 1) * depth, :],
                    preferred_element_type=F32,
                )
            cell = sigmoid(gates[:, chans : 2 * chans]) * cell + sigmoid(
                gates[:, :chans]
            ) * jnp.tanh(gates[:, 2 * chans : 3 * chans])
            hidden = sigmoid(gates[:, 3 * chans :]) * jnp.tanh(cell)
            hidden = hidden.reshape(rows_n, width, chans)
            column = start_column + lax.broadcasted_iota(jnp.int32, hidden.shape, 1)
            inside = jnp.logical_and(column >= 0, column < plan.grid_columns)
            hidden = jnp.where(inside, hidden, 0.0)
            extent = hidden_out.shape[2] if hidden_out is not None else width
            if extent < width:
                shift = plan.pad - (extent - plan.strip) // 2
                moved = pltpu.roll(hidden.reshape(total, chans), total - shift, 0)
                moved = moved.reshape(rows_n, width, chans)[:, :extent]
                hidden_out[step - first_step] = moved.astype(BF)
            elif hidden_out is not None:
                hidden_out[step - first_step] = hidden.astype(BF)
            hidden = hidden.astype(BF)
            keep(step, hidden)
        if cell_out is not None:
            cell_out[...] = cell
        if last_step == steps:
            keep(steps, cell.astype(BF).reshape(rows_n, width, chans))


def advance(plan, phase, first_step, last_step, feed, kept):
    vmem = pl.BlockSpec(memory_space=pltpu.VMEM)
    operands = [*feed, *kept]
    chunk = last_step - first_step
    extent = plan.extent(phase, first_step, last_step)
    outs = []
    if last_step < plan.steps or phase < plan.layers - 1:
        outs.append(jax.ShapeDtypeStruct((chunk, plan.rows_n, extent, plan.chans), BF))
    if last_step < plan.steps:
        outs.append(jax.ShapeDtypeStruct((plan.total, plan.chans), F32))
    if plan.lends(phase, first_step):
        outs.append(jax.ShapeDtypeStruct((plan.count * plan.lent_rows, plan.chans), BF))
    aliases = {len(feed) + n: len(outs) + n for n in range(len(kept))}
    outs += [jax.ShapeDtypeStruct(part.shape, part.dtype) for part in kept]
    return pl.pallas_call(
        functools.partial(chunk_kernel, plan, phase, first_step, last_step, len(kept)),
        out_shape=outs,
        in_specs=[vmem] * len(operands),
        out_specs=[vmem] * len(outs),
        scratch_shapes=[
            pltpu.VMEM((plan.total + 2 * plan.width, 6 * plan.chans), BF),
            pltpu.VMEM((plan.total, plan.chans), F32),
        ],
        input_output_aliases=aliases,
        compiler_params=pltpu.CompilerParams(vmem_limit_bytes=plan.room),
        cost_estimate=pl.CostEstimate(
            flops=2 * chunk * plan.total * 18 * plan.chans * 4 * plan.chans,
            bytes_accessed=1000000,
            transcendentals=5 * chunk * plan.total * plan.chans,
        ),
    )(*operands)


def merge_kernel(plan, *refs):
    maps_out, cell_out = refs[-2:]
    place = lax.axis_index("rows")
    for hop in range(plan.count):
        source = partner(place, hop_at(hop, plan.count), plan.count)[1]
        columns = pl.ds(pl.multiple_of(source * plan.strip, plan.strip), plan.strip)
        for number, (begin, end) in enumerate(plan.bounds):
            part = refs[number * plan.count + hop]
            for step in range(begin, min(end, plan.steps)):
                maps_out[0, step, :, columns, :] = part[:, step - begin]
            if end > plan.steps:
                cell_out[0, :, columns, :] = part[:, plan.steps - begin].astype(F32)


def pack(plan, arrays):
    vmem = pl.BlockSpec(memory_space=pltpu.VMEM)
    shape = (2 + plan.steps, plan.band, plan.columns + 2 * plan.edge, plan.chans)
    rows = [plan.early_rows] * plan.count + [plan.late_rows] * plan.count
    return pl.pallas_call(
        functools.partial(pack_kernel, plan),
        out_shape=[jax.ShapeDtypeStruct((extent, plan.chans), BF) for extent in rows],
        in_specs=[vmem] * len(arrays),
        out_specs=[vmem] * len(rows),
        scratch_shapes=[pltpu.VMEM(shape, F32)],
        compiler_params=pltpu.CompilerParams(vmem_limit_bytes=plan.room),
    )(*arrays)


def load_kernel(weights_in, bias_in, _, weights, bias, sems):
    copies = [
        pltpu.make_async_copy(weights_in, weights, sems.at[0]),
        pltpu.make_async_copy(bias_in, bias, sems.at[1]),
    ]
    for copy in copies:
        copy.start()
    for copy in copies:
        copy.wait()


def settle(plan, parts, kept):
    vmem = pl.BlockSpec(memory_space=pltpu.VMEM)
    return pl.pallas_call(
        lambda *refs: None,
        out_shape=jax.ShapeDtypeStruct(kept.shape, kept.dtype),
        in_specs=[vmem] * (1 + len(parts)),
        out_specs=vmem,
        input_output_aliases={len(parts): 0},
        compiler_params=pltpu.CompilerParams(vmem_limit_bytes=plan.room),
    )(*parts, kept)


def exchange(plan, pieces):
    got = [pieces[0]]
    for number in range(1, plan.count):
        route = []
        for row in range(plan.count):
            for col in range(plan.cols):
                hop = plan.count - number if SPREAD and col % 2 else number
                target = partner(row, hop, plan.count)[0]
                route.append((row * plan.cols + col, target * plan.cols + col))
        got.append(lax.ppermute(pieces[number], ("rows", "cols"), route))
    return got


def shards(inputs, hidden_init, cell_init, kernels, biases):
    plan = Plan(inputs)
    place = lax.axis_index("rows")
    steps, band, chans, count, layers = (
        plan.steps,
        plan.band,
        plan.chans,
        plan.count,
        plan.layers,
    )
    vmem = pl.BlockSpec(memory_space=pltpu.VMEM)
    params = pltpu.CompilerParams(vmem_limit_bytes=plan.room)
    maps = jnp.concatenate([hidden_init, cell_init.astype(BF), inputs], axis=0)
    if plan.cols == 2:
        beside = pl.pallas_call(
            functools.partial(edge_kernel, plan),
            out_shape=jax.ShapeDtypeStruct((2 + steps, band, plan.edge, chans), BF),
            in_specs=[vmem],
            out_specs=vmem,
            compiler_params=params,
        )(maps)
        left = right = lax.ppermute(beside, "cols", [(0, 1), (1, 0)])
    else:
        ring = [(n, (n + 1) % plan.cols) for n in range(plan.cols)]
        left = lax.ppermute(maps[:, :, plan.columns - plan.edge :], "cols", ring)
        right = lax.ppermute(maps[:, :, : plan.edge], "cols", [(b, a) for a, b in ring])
    packed = pack(plan, [maps, left, right])
    weights, bias = pl.pallas_call(
        load_kernel,
        out_shape=[jax.ShapeDtypeStruct(part.shape, part.dtype) for part in (kernels[0], biases)],
        in_specs=[pl.BlockSpec(memory_space=pltpu.HBM)] * 2 + [vmem],
        out_specs=[vmem] * 2,
        scratch_shapes=[pltpu.SemaphoreType.DMA((2,))],
        compiler_params=params,
    )(kernels[0], biases, packed[0])
    early = exchange(plan, packed[:count])
    late = exchange(plan, packed[count:])
    lent = []
    back = [(1, 0)] if LEND_ONE_WAY else [(n, (n - 1) % layers) for n in range(layers)]
    if plan.lent_steps and not LEND_AFTER:
        borrowed = jnp.concatenate([piece[: plan.lent_rows] for piece in early], axis=0)
        lent = [lax.ppermute(borrowed, "pipe", back)]

    kept = [
        jnp.zeros((plan.rows_n, end - begin, plan.width, chans), BF) for begin, end in plan.bounds
    ]

    def out_piece(part, hop):
        target = partner(place, hop_at(hop, count), count)[0]
        piece = lax.dynamic_slice_in_dim(part, target * band, band, axis=0)
        return piece[:, :, plan.pad : plan.pad + plan.strip]

    chunks = []
    while not chunks or chunks[-1][1] < steps:
        begin = chunks[-1][1] if chunks else 0
        size = CHUNKS[len(chunks)] if len(chunks) < len(CHUNKS) else 1
        chunks.append((begin, min(begin + size, steps)))
    order = sorted(
        (number + LAG * phase, -phase, number)
        for phase in range(layers)
        for number in range(len(chunks))
    )
    state = [[] for _ in range(layers)]
    sent = {}
    parts = []
    for _, minus_phase, number in order:
        phase = -minus_phase
        first_step, last_step = chunks[number]
        takes = needed(plan, phase, first_step, last_step)
        feed = []
        for wanted, arrays in zip(takes, (early, late, lent)):
            feed += arrays if wanted else []
        feed += [sent[phase - 1, number]] if phase > 0 else []
        feed += state[phase]
        results = advance(plan, phase, first_step, last_step, feed + [weights, bias], kept)
        results, kept = list(results[: -len(kept)]), list(results[-len(kept) :])
        if plan.lends(phase, first_step):
            lent = [lax.ppermute(results.pop(), "pipe", back)]
        if last_step < steps:
            state[phase] = results
        if phase < layers - 1:
            hidden = results[0]
            ring = [(n, (n + 1) % layers) for n in range(layers)]
            if HAND_ONE_WAY:
                ring = [(phase, phase + 1)]
            sent[phase, number] = lax.ppermute(hidden, "pipe", ring)
        if phase == layers - 1 and last_step >= plan.bounds[0][1] and len(kept) == 2:
            done = kept.pop(0)
            parts += exchange(plan, [out_piece(done, hop) for hop in range(count)])
    rest = settle(plan, parts[1:2], kept[0])
    parts += exchange(plan, [out_piece(rest, hop) for hop in range(count)])
    vmem = pl.BlockSpec(memory_space=pltpu.VMEM)
    return pl.pallas_call(
        functools.partial(merge_kernel, plan),
        out_shape=(
            jax.ShapeDtypeStruct((1, steps, band, plan.columns, chans), BF),
            jax.ShapeDtypeStruct((1, band, plan.columns, chans), F32),
        ),
        in_specs=[vmem] * len(parts),
        out_specs=(vmem, vmem),
        compiler_params=pltpu.CompilerParams(vmem_limit_bytes=plan.room),
    )(*parts)


def solution(mesh):
    return jax.shard_map(
        shards,
        mesh=mesh,
        in_specs=(
            P(None, ("groups", "rows"), "cols", None),
            P("pipe", ("groups", "rows"), "cols", None),
            P("pipe", ("groups", "rows"), "cols", None),
            P("pipe", None, None),
            P("pipe", None),
        ),
        out_specs=(
            P("pipe", None, ("groups", "rows"), "cols", None),
            P("pipe", ("groups", "rows"), "cols", None),
        ),
        check_vma=False,
    )
```

```python
import functools

import jax
import jax.numpy as jnp
from jax import lax
from jax.experimental import pallas as pl
from jax.experimental.pallas import tpu as pltpu
from jax.sharding import PartitionSpec as P

BF = jnp.bfloat16
F32 = jnp.float32
CHUNKS = (2, 2, 2, 2)
LAG = 3
FIRST = 2
LENT = 3
EARLY_OUT = 6
LEND_AFTER = False
SPREAD = True
LEND_ONE_WAY = True
HAND_ONE_WAY = True
MIB = 1024 * 1024


def round_up(value, unit):
    return -(-value // unit) * unit


def partner(index, hop, count):
    if count & (count - 1) == 0:
        return index ^ hop, index ^ hop
    return (index + hop) % count, (index + count - hop) % count


def hop_at(number, count):
    if not SPREAD or number == 0:
        return number
    return jnp.where(lax.axis_index("cols") % 2 == 0, number, count - number)


def sigmoid(value):
    return 0.5 * jnp.tanh(0.5 * value) + 0.5


class Piece:
    def __init__(self, strip, need, begin, band):
        self.extent = round_up(strip + 2 * need, 8)
        self.left = (self.extent - strip) // 2
        self.begin = begin
        self.end = begin + band * self.extent


class Plan:
    def __init__(self, inputs):
        self.steps, self.band, self.columns, self.chans = inputs.shape
        self.count = lax.axis_size("rows")
        self.cols = lax.axis_size("cols")
        self.layers = lax.axis_size("pipe")
        self.grid_columns = self.columns * self.cols
        self.rows_n = self.band * self.count
        self.strip = self.columns // self.count
        most = self.steps + self.layers - 1
        self.pad = round_up(most - 1, 8)
        self.width = round_up(self.strip + 2 * self.pad, 16)
        self.total = self.rows_n * self.width
        self.room = 4 * MIB + self.total * self.chans * (4 * 4 * 6 + 12)
        self.lent_steps = min(LENT, self.steps - 1) if self.layers > 1 else 0
        own = self.steps - self.lent_steps
        self.first = min(FIRST, own)
        needs = [most, most - 1] + [most - step for step in range(self.steps)]
        inputs_of = lambda begin, end: [2 + step for step in range(begin, end)]
        self.early, rows_a = self.pieces(needs, [0, 1] + inputs_of(0, self.first))
        self.late, rows_b = self.pieces(needs, inputs_of(self.first, own))
        self.lent, self.lent_rows = self.pieces(needs, inputs_of(own, self.steps))
        self.state, rows_c = self.pieces(needs, [0, 1])
        self.early_rows = max(rows_a, self.lent_rows)
        self.late_rows = max(rows_b, rows_c)
        half = min(EARLY_OUT, self.steps)
        self.bounds = [(0, half), (half, self.steps + 1)]
        self.edge = round_up(max((self.pieces(needs, [n])[0][n].left for n in range(len(needs)))) + 4, 16)

    def reach(self, phase, step):
        return (self.steps - 1 - step) + (self.layers - 1 - phase)

    def lends(self, phase, first_step):
        return LEND_AFTER and self.lent_steps > 0 and phase == 0 and first_step == 0

    def extent(self, phase, first_step, last_step):
        return min(round_up(self.strip + 2 * self.reach(phase, first_step), 8), self.width)

    def pieces(self, needs, numbers):
        found, begin = {}, 0
        for number in numbers:
            found[number] = Piece(self.strip, needs[number], begin, self.band)
            begin = found[number].end
        return found, begin


def edge_kernel(plan, maps, out):
    edge, columns = plan.edge, plan.columns

    @pl.when(lax.axis_index("cols") == 0)
    def _():
        out[...] = maps[:, :, columns - edge :]

    @pl.when(lax.axis_index("cols") != 0)
    def _():
        out[...] = maps[:, :, :edge]


def pack_kernel(plan, maps, left, right, *refs):
    early, late, padded = refs[: plan.count], refs[plan.count : -1], refs[-1]
    edge, columns, chans, band = plan.edge, plan.columns, plan.chans, plan.band
    place, col = lax.axis_index("rows"), lax.axis_index("cols")

    def fill(groups):
        for outs, pieces in groups:
            for number, piece in pieces.items():
                before = jnp.where(col > 0, left[number].astype(F32), 0.0)
                after = jnp.where(col < plan.cols - 1, right[number].astype(F32), 0.0)
                padded[number, :, 0:edge] = before
                padded[number, :, edge : edge + columns] = maps[number].astype(F32)
                padded[number, :, edge + columns : 2 * edge + columns] = after
        for outs, pieces in groups:
            for number, piece in pieces.items():
                for hop in range(plan.count):
                    target = partner(place, hop_at(hop, plan.count), plan.count)[0]
                    inset = edge - piece.left
                    rest = inset % 8
                    start = pl.multiple_of(target * plan.strip + (inset - rest), 8)
                    loaded = piece.extent + (8 if rest else 0)
                    value = padded[number, :, pl.ds(start, loaded), :]
                    if rest:
                        value = value.reshape(band * loaded, chans)
                        value = pltpu.roll(value, band * loaded - rest, 0)
                        value = value.reshape(band, loaded, chans)[:, : piece.extent]
                    value = value.reshape(band * piece.extent, chans)
                    outs[hop][piece.begin : piece.end] = value.astype(BF)

    @pl.when(lax.axis_index("pipe") == 0)
    def _():
        fill([(early, plan.early), (late, plan.late)])

    @pl.when(lax.axis_index("pipe") != 0)
    def _():
        fill([(early, plan.lent), (late, plan.state)])


def needed(plan, phase, first_step, last_step):
    if phase > 0:
        return [False, first_step == 0, False]
    own = plan.steps - plan.lent_steps
    return [
        first_step < plan.first,
        first_step < own and last_step > plan.first,
        last_step > own,
    ]


def chunk_kernel(plan, phase, first_step, last_step, parts, *refs):
    refs = list(refs)
    rows_n, band, width, chans = plan.rows_n, plan.band, plan.width, plan.chans
    count, total, steps = plan.count, plan.total, plan.steps
    early, late, lent = needed(plan, phase, first_step, last_step)
    early = [(refs.pop(0), 0) for _ in range(count)] if early else None
    late = [(refs.pop(0), 0) for _ in range(count)] if late else None
    if lent:
        lender = refs.pop(0)
        lent = [(lender, hop * plan.lent_rows) for hop in range(count)]
    maps_ref = None if phase == 0 else refs.pop(0)
    hidden_ref = cell_ref = None
    if first_step > 0:
        hidden_ref, cell_ref = refs.pop(0), refs.pop(0)
    weights, bias = refs[:2]
    outs, (slab, fresh) = refs[2 + parts : -2], refs[-2:]
    outs, kept = list(outs[:-parts]), outs[-parts:]
    hidden_out = outs.pop(0) if last_step < steps or phase < plan.layers - 1 else None
    cell_out = outs.pop(0) if last_step < steps else None
    if plan.lends(phase, first_step):
        borrowed = outs.pop(0)

        @pl.when(lax.axis_index("pipe") != phase)
        def _():
            for hop in range(count):
                begin = hop * plan.lent_rows
                borrowed[begin : begin + plan.lent_rows] = early[hop][0][: plan.lent_rows]

    bounds = plan.bounds[-len(kept) :]

    def keep(at, value):
        for ref, (begin, end) in zip(kept, bounds):
            if begin <= at < end:
                ref[:, at - begin] = value

    @pl.when(lax.axis_index("pipe") == phase)
    def _():
        place = lax.axis_index("rows")
        sources = [partner(place, hop_at(hop, count), count)[1] for hop in range(count)]
        start_column = (
            lax.axis_index("cols") * plan.columns + place * plan.strip - plan.pad
        )
        blank = jnp.zeros((width, 6 * chans), BF)
        slab[0:width, :] = blank
        slab[total + width : total + 2 * width, :] = blank

        def spread(lane, value):
            value = value.astype(F32)
            extent = value.shape[1]
            left = plan.pad if extent == width else (extent - plan.strip) // 2
            if extent < width:
                fill = jnp.zeros((rows_n, width - extent, chans), F32)
                value = jnp.concatenate([value, fill], axis=1)
            value = value.reshape(total, chans)
            for tap in range(3):
                shift = (plan.pad - left + 1 - tap) % total
                moved = pltpu.roll(value, shift, 0) if shift else value
                at = 2 * chans * tap + lane
                slab[width : width + total, at : at + chans] = moved.astype(BF)

        def bands(lane, refs_in, piece):
            for hop in range(count):
                ref, offset = refs_in[hop]
                flat = ref[offset + piece.begin : offset + piece.end].astype(F32)
                extent = piece.extent
                if extent < width:
                    flat = flat.reshape(band, extent, chans)
                    fill = jnp.zeros((band, width - extent, chans), F32)
                    flat = jnp.concatenate([flat, fill], axis=1).reshape(band * width, chans)
                    extent = width
                source = sources[hop]
                for tap in range(3) if lane is not None else (1,):
                    shift = (plan.pad - piece.left + 1 - tap) % (band * extent)
                    moved = pltpu.roll(flat, shift, 0) if shift else flat
                    moved = moved.reshape(band, extent, chans)[:, :width]
                    moved = moved.reshape(band * width, chans)
                    if lane is None:
                        start = pl.multiple_of(source * band * width, 16)
                        fresh[pl.ds(start, band * width), :] = moved
                    else:
                        at = 2 * chans * tap + lane
                        start = pl.multiple_of((source * band + 1) * width, 16)
                        slab[pl.ds(start, band * width), at : at + chans] = moved.astype(BF)

        hidden = None
        cell = None
        for step in range(first_step, last_step):
            if step == 0:
                pieces, from_refs = (plan.state, late) if phase > 0 else (plan.early, early)
                bands(chans, from_refs, pieces[0])
                bands(None, from_refs, pieces[1])
                cell = fresh[...]
            elif step == first_step:
                spread(chans, hidden_ref[hidden_ref.shape[0] - 1])
                cell = cell_ref[...]
            else:
                spread(chans, hidden)
            if phase > 0:
                spread(0, maps_ref[step - first_step])
            elif step < plan.first:
                bands(0, early, plan.early[2 + step])
            elif step < steps - plan.lent_steps:
                bands(0, late, plan.late[2 + step])
            else:
                bands(0, lent, plan.lent[2 + step])

            depth = 6 * chans
            gates = bias[0:1]
            for tap in range(3):
                gates = gates + jnp.dot(
                    slab[tap * width : tap * width + total, :],
                    weights[tap * depth : (tap + 1) * depth, :],
                    preferred_element_type=F32,
                )
            cell = sigmoid(gates[:, chans : 2 * chans]) * cell + sigmoid(
                gates[:, :chans]
            ) * jnp.tanh(gates[:, 2 * chans : 3 * chans])
            hidden = sigmoid(gates[:, 3 * chans :]) * jnp.tanh(cell)
            hidden = hidden.reshape(rows_n, width, chans)
            column = start_column + lax.broadcasted_iota(jnp.int32, hidden.shape, 1)
            inside = jnp.logical_and(column >= 0, column < plan.grid_columns)
            hidden = jnp.where(inside, hidden, 0.0)
            extent = hidden_out.shape[2] if hidden_out is not None else width
            if extent < width:
                shift = plan.pad - (extent - plan.strip) // 2
                moved = pltpu.roll(hidden.reshape(total, chans), total - shift, 0)
                moved = moved.reshape(rows_n, width, chans)[:, :extent]
                hidden_out[step - first_step] = moved.astype(BF)
            elif hidden_out is not None:
                hidden_out[step - first_step] = hidden.astype(BF)
            hidden = hidden.astype(BF)
            keep(step, hidden)
        if cell_out is not None:
            cell_out[...] = cell
        if last_step == steps:
            keep(steps, cell.astype(BF).reshape(rows_n, width, chans))


def advance(plan, phase, first_step, last_step, feed, kept):
    vmem = pl.BlockSpec(memory_space=pltpu.VMEM)
    operands = [*feed, *kept]
    chunk = last_step - first_step
    extent = plan.extent(phase, first_step, last_step)
    outs = []
    if last_step < plan.steps or phase < plan.layers - 1:
        outs.append(jax.ShapeDtypeStruct((chunk, plan.rows_n, extent, plan.chans), BF))
    if last_step < plan.steps:
        outs.append(jax.ShapeDtypeStruct((plan.total, plan.chans), F32))
    if plan.lends(phase, first_step):
        outs.append(jax.ShapeDtypeStruct((plan.count * plan.lent_rows, plan.chans), BF))
    aliases = {len(feed) + n: len(outs) + n for n in range(len(kept))}
    outs += [jax.ShapeDtypeStruct(part.shape, part.dtype) for part in kept]
    return pl.pallas_call(
        functools.partial(chunk_kernel, plan, phase, first_step, last_step, len(kept)),
        out_shape=outs,
        in_specs=[vmem] * len(operands),
        out_specs=[vmem] * len(outs),
        scratch_shapes=[
            pltpu.VMEM((plan.total + 2 * plan.width, 6 * plan.chans), BF),
            pltpu.VMEM((plan.total, plan.chans), F32),
        ],
        input_output_aliases=aliases,
        compiler_params=pltpu.CompilerParams(vmem_limit_bytes=plan.room),
        cost_estimate=pl.CostEstimate(
            flops=2 * chunk * plan.total * 18 * plan.chans * 4 * plan.chans,
            bytes_accessed=1000000,
            transcendentals=5 * chunk * plan.total * plan.chans,
        ),
    )(*operands)


def merge_kernel(plan, *refs):
    maps_out, cell_out = refs[-2:]
    place = lax.axis_index("rows")
    for hop in range(plan.count):
        source = partner(place, hop_at(hop, plan.count), plan.count)[1]
        columns = pl.ds(pl.multiple_of(source * plan.strip, plan.strip), plan.strip)
        for number, (begin, end) in enumerate(plan.bounds):
            part = refs[number * plan.count + hop]
            for step in range(begin, min(end, plan.steps)):
                maps_out[0, step, :, columns, :] = part[:, step - begin]
            if end > plan.steps:
                cell_out[0, :, columns, :] = part[:, plan.steps - begin].astype(F32)


def pack(plan, arrays):
    vmem = pl.BlockSpec(memory_space=pltpu.VMEM)
    shape = (2 + plan.steps, plan.band, plan.columns + 2 * plan.edge, plan.chans)
    rows = [plan.early_rows] * plan.count + [plan.late_rows] * plan.count
    return pl.pallas_call(
        functools.partial(pack_kernel, plan),
        out_shape=[jax.ShapeDtypeStruct((extent, plan.chans), BF) for extent in rows],
        in_specs=[vmem] * len(arrays),
        out_specs=[vmem] * len(rows),
        scratch_shapes=[pltpu.VMEM(shape, F32)],
        compiler_params=pltpu.CompilerParams(vmem_limit_bytes=plan.room),
    )(*arrays)


def load_kernel(weights_in, bias_in, _, weights, bias, sems):
    copies = [
        pltpu.make_async_copy(weights_in, weights, sems.at[0]),
        pltpu.make_async_copy(bias_in, bias, sems.at[1]),
    ]
    for copy in copies:
        copy.start()
    for copy in copies:
        copy.wait()


def settle(plan, parts, kept):
    vmem = pl.BlockSpec(memory_space=pltpu.VMEM)
    return pl.pallas_call(
        lambda *refs: None,
        out_shape=jax.ShapeDtypeStruct(kept.shape, kept.dtype),
        in_specs=[vmem] * (1 + len(parts)),
        out_specs=vmem,
        input_output_aliases={len(parts): 0},
        compiler_params=pltpu.CompilerParams(vmem_limit_bytes=plan.room),
    )(*parts, kept)


def exchange(plan, pieces):
    got = [pieces[0]]
    for number in range(1, plan.count):
        route = []
        for row in range(plan.count):
            for col in range(plan.cols):
                hop = plan.count - number if SPREAD and col % 2 else number
                target = partner(row, hop, plan.count)[0]
                route.append((row * plan.cols + col, target * plan.cols + col))
        got.append(lax.ppermute(pieces[number], ("rows", "cols"), route))
    return got


def shards(inputs, hidden_init, cell_init, kernels, biases):
    plan = Plan(inputs)
    place = lax.axis_index("rows")
    steps, band, chans, count, layers = (
        plan.steps,
        plan.band,
        plan.chans,
        plan.count,
        plan.layers,
    )
    vmem = pl.BlockSpec(memory_space=pltpu.VMEM)
    params = pltpu.CompilerParams(vmem_limit_bytes=plan.room)
    maps = jnp.concatenate([hidden_init, cell_init.astype(BF), inputs], axis=0)
    if plan.cols == 2:
        beside = pl.pallas_call(
            functools.partial(edge_kernel, plan),
            out_shape=jax.ShapeDtypeStruct((2 + steps, band, plan.edge, chans), BF),
            in_specs=[vmem],
            out_specs=vmem,
            compiler_params=params,
        )(maps)
        left = right = lax.ppermute(beside, "cols", [(0, 1), (1, 0)])
    else:
        ring = [(n, (n + 1) % plan.cols) for n in range(plan.cols)]
        left = lax.ppermute(maps[:, :, plan.columns - plan.edge :], "cols", ring)
        right = lax.ppermute(maps[:, :, : plan.edge], "cols", [(b, a) for a, b in ring])
    packed = pack(plan, [maps, left, right])
    weights, bias = pl.pallas_call(
        load_kernel,
        out_shape=[jax.ShapeDtypeStruct(part.shape, part.dtype) for part in (kernels[0], biases)],
        in_specs=[pl.BlockSpec(memory_space=pltpu.HBM)] * 2 + [vmem],
        out_specs=[vmem] * 2,
        scratch_shapes=[pltpu.SemaphoreType.DMA((2,))],
        compiler_params=params,
    )(kernels[0], biases, packed[0])
    early = exchange(plan, packed[:count])
    late = exchange(plan, packed[count:])
    lent = []
    back = [(1, 0)] if LEND_ONE_WAY else [(n, (n - 1) % layers) for n in range(layers)]
    if plan.lent_steps and not LEND_AFTER:
        borrowed = jnp.concatenate([piece[: plan.lent_rows] for piece in early], axis=0)
        lent = [lax.ppermute(borrowed, "pipe", back)]

    kept = [
        jnp.zeros((plan.rows_n, end - begin, plan.width, chans), BF) for begin, end in plan.bounds
    ]

    def out_piece(part, hop):
        target = partner(place, hop_at(hop, count), count)[0]
        piece = lax.dynamic_slice_in_dim(part, target * band, band, axis=0)
        return piece[:, :, plan.pad : plan.pad + plan.strip]

    chunks = []
    while not chunks or chunks[-1][1] < steps:
        begin = chunks[-1][1] if chunks else 0
        size = CHUNKS[len(chunks)] if len(chunks) < len(CHUNKS) else 1
        chunks.append((begin, min(begin + size, steps)))
    order = sorted(
        (number + LAG * phase, -phase, number)
        for phase in range(layers)
        for number in range(len(chunks))
    )
    state = [[] for _ in range(layers)]
    sent = {}
    parts = []
    for _, minus_phase, number in order:
        phase = -minus_phase
        first_step, last_step = chunks[number]
        takes = needed(plan, phase, first_step, last_step)
        feed = []
        for wanted, arrays in zip(takes, (early, late, lent)):
            feed += arrays if wanted else []
        feed += [sent[phase - 1, number]] if phase > 0 else []
        feed += state[phase]
        results = advance(plan, phase, first_step, last_step, feed + [weights, bias], kept)
        results, kept = list(results[: -len(kept)]), list(results[-len(kept) :])
        if plan.lends(phase, first_step):
            lent = [lax.ppermute(results.pop(), "pipe", back)]
        if last_step < steps:
            state[phase] = results
        if phase < layers - 1:
            hidden = results[0]
            ring = [(n, (n + 1) % layers) for n in range(layers)]
            if HAND_ONE_WAY:
                ring = [(phase, phase + 1)]
            sent[phase, number] = lax.ppermute(hidden, "pipe", ring)
        if phase == layers - 1 and last_step >= plan.bounds[0][1] and len(kept) == 2:
            done = kept.pop(0)
            parts += exchange(plan, [out_piece(done, hop) for hop in range(count)])
    rest = settle(plan, parts[1:2], kept[0])
    parts += exchange(plan, [out_piece(rest, hop) for hop in range(count)])
    vmem = pl.BlockSpec(memory_space=pltpu.VMEM)
    return pl.pallas_call(
        functools.partial(merge_kernel, plan),
        out_shape=(
            jax.ShapeDtypeStruct((1, steps, band, plan.columns, chans), BF),
            jax.ShapeDtypeStruct((1, band, plan.columns, chans), F32),
        ),
        in_specs=[vmem] * len(parts),
        out_specs=(vmem, vmem),
        compiler_params=pltpu.CompilerParams(vmem_limit_bytes=plan.room),
    )(*parts)


def solution(mesh):
    return jax.shard_map(
        shards,
        mesh=mesh,
        in_specs=(
            P(None, ("groups", "rows"), "cols", None),
            P("pipe", ("groups", "rows"), "cols", None),
            P("pipe", ("groups", "rows"), "cols", None),
            P("pipe", None, None),
            P("pipe", None),
        ),
        out_specs=(
            P("pipe", None, ("groups", "rows"), "cols", None),
            P("pipe", ("groups", "rows"), "cols", None),
        ),
        check_vma=False,
    )
```
